128 devices in a mesh: users: 8 (over z, x_lo), srow: 4 (over y), scol: 4 (over x_hi, core).
Axes of the slice: x: 4 (x_hi: 2, x_lo: 2; x = x_hi * 2 + x_lo), y: 4, z: 4, core: 2. Of those that a mesh axis runs over, the one named last changes fastest.
Arguments:
- history: bfloat16 [8192, 65536], P('users', ('srow', 'scol')), as said below
- ridge: float32 [65536], replicated, may hold values from 0.2 to 2
- pivot_inverse: float32 [2, 1024, 1024], replicated, as said below
- panel_ids: int32 [2], replicated, may hold values from 0 to 63, as said below
Outputs:
- factor_first: float32 [16, 4096, 1024], P(('srow', 'scol'), 'users')
- factor_second: float32 [16, 4096, 1024], P(('srow', 'scol'), 'users')
The draws below stay inside these ranges and needn't reach their ends.
Inputs may be any that keep to these rules, and one draw needn't show every extreme that they name: `history`: about a third of the entries are nonzero; users and items have scales spread over a factor of ten. `pivot_inverse`: each matrix has a positive diagonal and small entries off it. `panel_ids`: 2 distinct panel numbers; the last panel is always among them.
All inputs are finite; a program needn't handle non-finite values.
Results may differ from the reference program's by a relative error of at most 0.0003.
Values may be sent and summed in bfloat16 or wider, within the bound.
A program may use at most 192 MiB of HBM per device.

```python
import math
import jax
import jax.numpy as jnp
from jax import lax

ITEMS = 65536
PB = 1024
NPAN = 2
ROWS = 8192
GROUPS = 16


def draw_history(key, part):
    key = jax.random.fold_in(key, 11)
    keys = jax.random.split(key, 4)
    user_scale = jnp.exp(jax.random.uniform(keys[0], (ROWS, 1), jnp.float32, jnp.log(0.3), jnp.log(3.0)))
    item_scale = jnp.exp(jax.random.uniform(keys[1], (1, ITEMS), jnp.float32, jnp.log(0.3), jnp.log(3.0)))
    live = jax.random.uniform(keys[2], (ROWS, ITEMS), jnp.float32) < 0.35
    values = jax.random.normal(keys[3], (ROWS, ITEMS), jnp.float32)
    return jnp.where(live, values * user_scale * item_scale, 0.0).astype(jnp.bfloat16)


def draw_pivot_inverse(key, part):
    key = jax.random.fold_in(key, 23)
    keys = jax.random.split(key, 2)
    diagonal = jnp.exp(jax.random.uniform(keys[0], (NPAN, 1, PB), jnp.float32, jnp.log(0.2), jnp.log(1.0)))
    spread = 0.25 * jax.random.normal(keys[1], (NPAN, PB, PB), jnp.float32) / jnp.sqrt(jnp.float32(PB))
    row_index = jnp.arange(PB, dtype=jnp.int32)[:, None]
    col_index = jnp.arange(PB, dtype=jnp.int32)[None, :]
    identity = (row_index == col_index).astype(jnp.float32)[None, :, :]
    return (identity * diagonal + spread).astype(jnp.float32)


def draw_panel_ids(key, part):
    key = jax.random.fold_in(key, 37)
    keys = jax.random.split(key, 2)
    last_panel = ITEMS // PB - 1
    others = jax.random.permutation(keys[0], last_panel)[:NPAN - 1].astype(jnp.int32)
    place = jax.random.randint(keys[1], (), 0, NPAN, dtype=jnp.int32)
    positions = jnp.arange(NPAN, dtype=jnp.int32)
    source = jnp.where(positions < place, positions, positions - 1)
    source = jnp.clip(source, 0, NPAN - 2)
    picked = others[source]
    return jnp.where(positions == place, jnp.int32(last_panel), picked).astype(jnp.int32)


def setup_inputs(seed: int = 0) -> dict:
    key_of = jax.random.split(jax.random.key(seed), 5)
    return {
        "history": draw_history(jax.random.fold_in(key_of[4], 71), 0),
        "ridge": jnp.clip(jnp.exp(jax.random.uniform(key_of[1], (ITEMS,), jnp.float32, math.log(0.2), math.log(2.0))), 0.2, 2.0),
        "pivot_inverse": draw_pivot_inverse(jax.random.fold_in(key_of[4], 71), 0),
        "panel_ids": draw_panel_ids(jax.random.fold_in(key_of[4], 71), 0),
    }


def reference(history, ridge, pivot_inverse, panel_ids):
    total_rows = history.shape[0]
    item_count = history.shape[1]
    panel_width = pivot_inverse.shape[1]
    item_index = jnp.arange(item_count, dtype=jnp.int32)
    gram_list = []
    for panel_step in range(NPAN):
        start_item = (panel_ids[panel_step] * panel_width).astype(jnp.int32)
        panel_hist = lax.dynamic_slice_in_dim(history, start_item, panel_width, 1)
        gram_cols = jnp.dot(history.T, panel_hist, preferred_element_type=jnp.float32) / float(total_rows)
        column_items = start_item + jnp.arange(panel_width, dtype=jnp.int32)
        on_diagonal = item_index[:, None] == column_items[None, :]
        gram_cols = gram_cols + jnp.where(on_diagonal, ridge[:, None], jnp.float32(0.0))
        gram_list.append(gram_cols)
    factor_a = jnp.dot(gram_list[0], pivot_inverse[0], precision=lax.Precision.HIGHEST)
    second_start = (panel_ids[1] * panel_width).astype(jnp.int32)
    pivot_rows = lax.dynamic_slice_in_dim(gram_list[0], second_start, panel_width, 0)
    schur = gram_list[1] - jnp.dot(factor_a, pivot_rows.T, precision=lax.Precision.HIGHEST)
    factor_b = jnp.dot(schur, pivot_inverse[1], precision=lax.Precision.HIGHEST)
    shape_out = (GROUPS, item_count // GROUPS, panel_width)
    return factor_a.reshape(shape_out), factor_b.reshape(shape_out)
```

```python
import functools

import jax
import jax.numpy as jnp
from jax import lax
from jax.experimental import pallas as pl
from jax.experimental.pallas import tpu as pltpu
from jax.sharding import PartitionSpec as P

MESH = pl.DeviceIdType.MESH
F32 = jnp.float32
BF16 = jnp.bfloat16
I16 = jnp.int16

CW = 256
KINDS = "ZXZXZXZZ"
NCH = len(KINDS)
TOP = 32767.0


def encode(v):
    top = jnp.maximum(jnp.max(jnp.abs(v), axis=0, keepdims=True), 1e-30)
    q = jnp.round(v * (TOP / top)).astype(jnp.int32).astype(I16)
    return q, top * (1.0 / TOP)


def decode(q, s):
    return q.astype(jnp.int32).astype(F32) * s


def kernel(pid, hist_hbm, gram_out, piv_out,
           hist, pT, msk, cor, comb, yin, mid, xin,
           q2, s2, qd, sd, qa, sa, qx, sx,
           r2, t2, rd, td, ra, ta, rx, tx, keep,
           pvp, pvr, pvs,
           bs, br, zs, zr, xs, xr, ps, pr, hs):
    u = lax.axis_index("users")
    y = lax.axis_index("srow")
    s = lax.axis_index("scol")
    z, xl = u // 2, u % 2
    xh, co = s // 2, s % 2
    g = y * 4 + s
    users, items = hist.shape
    zc = items // 4
    half = zc // 2

    def at(z_=None, xl_=None, y_=None, xh_=None, co_=None):
        zz = z if z_ is None else z_
        ll = xl if xl_ is None else xl_
        yy = y if y_ is None else y_
        hh = xh if xh_ is None else xh_
        cc = co if co_ is None else co_
        return (zz * 2 + ll, yy, hh * 2 + cc)

    up, dn, op = (z + 1) % 4, (z + 3) % 4, (z + 2) % 4
    p_up, p_dn, p_x = at(z_=up), at(z_=dn), at(xl_=1 - xl)
    p_core, p_xh = at(co_=1 - co), at(xh_=1 - xh)
    p_y = [at(y_=(y + d) % 4) for d in (1, 2, 3)]
    p_u = [((u + d) % 8, y, s) for d in range(1, 8)]

    load = pltpu.make_async_copy(hist_hbm, hist, hs)
    load.start()
    barrier = pltpu.get_barrier_semaphore()
    everyone = [p_core, p_xh] + p_y + p_u
    for peer in everyone:
        pl.semaphore_signal(barrier, inc=1, device_id=peer, device_id_type=MESH)
    pl.semaphore_wait(barrier, len(everyone))
    load.wait()

    live = {}

    def send(key, src, dst, ss, rs, peer):
        c = pltpu.make_async_remote_copy(src, dst, ss, rs, device_id=peer, device_id_type=MESH)
        c.start()
        live[key] = c

    sent = []

    def got(key):
        c = live.pop(key)
        c.wait_recv()
        sent.append(c)

    def drop(key):
        for c in [c for c in sent if getattr(c, "tag", None) == key]:
            c.wait_send()

    def bc1(c):
        k, j = divmod(c, NCH // 2)
        v = None
        for b in range(4):
            mine = (pid[k] == 4 * g + b).astype(F32).astype(BF16)
            term = hist[:, pl.ds(b * 1024 + j * CW, CW)] * mine
            v = term if v is None else v + term
        msk[c] = v.T
        send(("b0", c), msk.at[c, pl.ds((1 - co) * 128, 128)], cor.at[c], bs.at[c, 0], br.at[c, 0], p_core)

    def bc2(c):
        got(("b0", c))
        comb[c] = msk[c, pl.ds(pl.multiple_of(co * 128, 128), 128)] + cor[c]
        for d in (1, 2, 3):
            yy = (y + d) % 4
            send(("b1", c, d), comb.at[c, pl.ds(pl.multiple_of(yy * 32, 32), 32)], yin.at[c, d - 1],
                 bs.at[c, d], br.at[c, d], p_y[d - 1])

    def bc3(c):
        for d in (1, 2, 3):
            got(("b1", c, d))
        mid[c] = comb[c, pl.ds(pl.multiple_of(y * 32, 32), 32)] + yin[c, 0] + yin[c, 1] + yin[c, 2]
        send(("b2", c), mid.at[c], xin.at[c], bs.at[c, 4], br.at[c, 4], p_xh)

    def bc4(c):
        got(("b2", c))
        here = pl.ds(pl.multiple_of(co * 128 + y * 32, 32), 32)
        pT[c, here] = mid[c] + xin[c]
        for d in (1, 2, 3):
            send(("b3", c, d), pT.at[c, here], pT.at[c, here], bs.at[c, 4 + d], br.at[c, 4 + d], p_y[d - 1])

    def bc5(c):
        for d in (1, 2, 3):
            got(("b3", c, d))
        here = pl.ds(pl.multiple_of(co * 128, 128), 128)
        send(("b4", c), pT.at[c, here], pT.at[c, here], bs.at[c, 8], br.at[c, 8], p_core)

    def bc6(c):
        got(("b4", c))

    def tiles(c, lane0, width, adds, out):
        def one(t, carry):
            lane = pl.multiple_of(lane0 + t * 256, 256)
            o = pl.multiple_of(t * 256, 256)
            v = jnp.dot(pT[c], hist[:, pl.ds(lane, 256)], preferred_element_type=F32)
            for q, sc in adds:
                v = v + decode(q[:, pl.ds(o, 256)], sc[:, pl.ds(o, 256)])
            out(o, v)
            return carry
        if width == 256:
            one(0, 0)
        else:
            lax.fori_loop(0, width // 256, one, 0)

    def coded(qb, sb):
        def out(o, v):
            q, sc = encode(v)
            qb[:, pl.ds(o, 256)] = q
            sb[:, pl.ds(o, 256)] = sc
        return out

    def sendq(key, q, sc, rq, rsc, ss, rs, i, peer):
        send(key + ("q",), q, rq, ss.at[i], rs.at[i], peer)
        send(key + ("s",), sc, rsc, ss.at[i + 1], rs.at[i + 1], peer)

    def gotq(key):
        got(key + ("q",))
        got(key + ("s",))

    def hw(c):
        return half if KINDS[c] == "Z" else half // 2

    def lane(c, zz, h):
        if KINDS[c] == "Z":
            return zz * zc + h * half
        return zz * zc + xl * half + h * (half // 2)

    def xadd(c, zz_i, h):
        if KINDS[c] == "Z":
            return []
        w = half // 2
        return [(rx.at[c, zz_i, :, pl.ds(h * w, w)], tx.at[c, zz_i, :, pl.ds(h * w, w)])]

    def x1(c):
        p = c % 2
        for i, zz in enumerate((op, up, dn, z)):
            if c >= 2:
                for kk in ("q", "s"):
                    wait_sent(("x", c - 2, i, kk))
            tiles(c, zz * zc + (1 - xl) * half, half, [], coded(qx.at[p, i], sx.at[p, i]))
            sendq(("x", c, i), qx.at[p, i], sx.at[p, i], rx.at[c, i], tx.at[c, i], xs.at[c], xr.at[c], 2 * i, p_x)

    waited = set()

    def wait_sent(key):
        if key in waited or key not in descs:
            return
        waited.add(key)
        descs[key].wait_send()

    descs = {}
    _send = send

    def send(key, *a):
        _send(key, *a)
        descs[key] = live[key]

    def z_first(c):
        p = c % 2
        w = hw(c)
        if KINDS[c] == "X":
            gotq(("x", c, 0))
        for h, peer in ((0, p_dn), (1, p_up)):
            for kk in ("q", "s"):
                wait_sent(("z2", c - 2, h, kk))
            qb, sb = q2.at[p, h, :, pl.ds(0, w)], s2.at[p, h, :, pl.ds(0, w)]
            tiles(c, lane(c, op, h), w, xadd(c, 0, h), coded(qb, sb))
            sendq(("z2", c, h), qb, sb, r2.at[c, h, :, pl.ds(0, w)], t2.at[c, h, :, pl.ds(0, w)], zs.at[c], zr.at[c], 2 * h, peer)

    def z_direct(c):
        p = c % 2
        w = hw(c)
        if KINDS[c] == "X":
            gotq(("x", c, 1))
            gotq(("x", c, 2))
        for h, zz, i, peer in ((0, up, 1, p_up), (1, dn, 2, p_dn)):
            for kk in ("q", "s"):
                wait_sent(("zd", c - 2, h, kk))
            qb, sb = qd.at[p, h, :, pl.ds(0, w)], sd.at[p, h, :, pl.ds(0, w)]
            tiles(c, lane(c, zz, h), w, xadd(c, i, h), coded(qb, sb))
            sendq(("zd", c, h), qb, sb, rd.at[c, h, :, pl.ds(0, w)], td.at[c, h, :, pl.ds(0, w)], zs.at[c], zr.at[c], 4 + 2 * h, peer)

    def z_pass(c):
        p = c % 2
        w = hw(c)
        for h, zz, i, peer in ((0, dn, 2, p_dn), (1, up, 1, p_up)):
            gotq(("z2", c, h))
            for kk in ("q", "s"):
                wait_sent(("za", c - 2, h, kk))
            qb, sb = qa.at[p, h, :, pl.ds(0, w)], sa.at[p, h, :, pl.ds(0, w)]
            adds = xadd(c, i, h) + [(r2.at[c, h, :, pl.ds(0, w)], t2.at[c, h, :, pl.ds(0, w)])]
            tiles(c, lane(c, zz, h), w, adds, coded(qb, sb))
            sendq(("za", c, h), qb, sb, ra.at[c, h, :, pl.ds(0, w)], ta.at[c, h, :, pl.ds(0, w)], zs.at[c], zr.at[c], 8 + 2 * h, peer)

    def z_last(c):
        p = c % 2
        w = hw(c)
        if KINDS[c] == "X":
            gotq(("x", c, 3))
        for h in (0, 1):
            gotq(("zd", c, h))
            gotq(("za", c, h))
        if KINDS[c] == "X":
            for h in (0, 1):
                adds = xadd(c, 3, h) + [(b.at[c, h, :, pl.ds(0, w)], t.at[c, h, :, pl.ds(0, w)]) for b, t in ((rd, td), (ra, ta))]

                def out(o, v, h=h):
                    gram_out[c, :, pl.ds(h * w + o, 256)] = v
                tiles(c, lane(c, z, h), w, adds, out)
            return

        def adds(h):
            return [(b.at[c, h], t.at[c, h]) for b, t in ((rd, td), (ra, ta))]

        for kk in ("q", "s"):
            wait_sent(("x", c - 2, 0, kk))
        tiles(c, lane(c, z, 1 - xl), w, adds(1 - xl), coded(qx.at[p, 0], sx.at[p, 0]))
        sendq(("x", c, 0), qx.at[p, 0], sx.at[p, 0], rx.at[c, 0], tx.at[c, 0], xs.at[c], xr.at[c], 0, p_x)

        def out(o, v):
            keep[p, :, pl.ds(o, 256)] = v
        tiles(c, lane(c, z, xl), w, adds(xl), out)

    def x_last(c):
        p = c % 2
        gotq(("x", c, 0))

        def one(t, carry):
            o = pl.multiple_of(t * 256, 256)
            gram_out[c, :, pl.ds(o, 256)] = keep[p, :, pl.ds(o, 256)] + decode(
                rx[c, 0, :, pl.ds(o, 256)], tx[c, 0, :, pl.ds(o, 256)])
            return carry
        lax.fori_loop(0, half // 256, one, 0)

    def pv1():
        rows = pT[NCH // 2 + g // 4, pl.ds(pl.multiple_of((g % 4) * 64, 64), 64)]
        for j in range(NCH // 2):
            pvp[:, pl.ds(j * CW, CW)] = lax.dot_general(
                rows, pT[j], (((1,), (1,)), ((), ())), preferred_element_type=F32)
        for d in range(1, 8):
            uu = (u + d) % 8
            send(("p0", d), pvp.at[pl.ds(pl.multiple_of(uu * 8, 8), 8)], pvr.at[d - 1], ps.at[d - 1], pr.at[d - 1], p_u[d - 1])

    def pv2():
        v = pvp[pl.ds(pl.multiple_of(u * 8, 8), 8)]
        for d in range(1, 8):
            got(("p0", d))
            v = v + pvr[d - 1]
        here = pl.ds(pl.multiple_of(u * 8, 8), 8)
        pvs[g, here] = v
        for d in range(1, 8):
            send(("p1", d), pvs.at[g, here], pvs.at[g, here], ps.at[6 + d], pr.at[6 + d], p_u[d - 1])

    def pv3():
        for d in range(1, 8):
            got(("p1", d))
        send(("p2",), pvs.at[g], pvs.at[g], ps.at[14], pr.at[14], p_xh)

    def pv4():
        got(("p2",))
        for d in (1, 2, 3):
            for b in (0, 1):
                gg = y * 4 + b * 2 + co
                send(("p3", d, b), pvs.at[gg], pvs.at[gg], ps.at[13 + 2 * d + b], pr.at[13 + 2 * d + b], p_y[d - 1])

    def pv5():
        for d in (1, 2, 3):
            for b in (0, 1):
                got(("p3", d, b))
        for b in range(8):
            gg = b * 2 + co
            send(("p4", b), pvs.at[gg], pvs.at[gg], ps.at[21 + b], pr.at[21 + b], p_core)

    def pv6():
        for b in range(8):
            got(("p4", b))
        piv_out[...] = pvs[...]

    bc = (bc1, bc2, bc3, bc4, bc5, bc6)
    for f in bc:
        f(0)
        f(1)
    side = [functools.partial(f, c) for c0 in (2, 4, 6) for f in bc for c in (c0, c0 + 1)]
    side += [pv1, pv2, pv3, pv4, pv5, pv6]
    side.reverse()

    def aside(n):
        for _ in range(n):
            if side:
                side.pop()()

    for i in range(NCH + 3):
        todo = []
        for lag in range(4):
            c = i - lag
            if not 0 <= c < NCH:
                continue
            if KINDS[c] == "Z":
                todo += [(z_first, z_direct), (z_pass,), (z_last,), (x_last,)][lag]and [
                    functools.partial(f, c) for f in [(z_first, z_direct), (z_pass,), (z_last,), (x_last,)][lag]]
            else:
                todo += [functools.partial(f, c) for f in [(x1,), (z_first, z_direct), (z_pass,), (z_last,)][lag]]
        for f in todo:
            f()
            aside(3)
    aside(len(side))
    for key, c in descs.items():
        if key not in waited:
            c.wait_send()


def run(history, panel_ids):
    users, items = history.shape
    half = items // 8
    vm = pltpu.VMEM
    dma = pltpu.SemaphoreType.DMA
    scratch = [
        vm((users, items), BF16), vm((NCH, CW, users), BF16), vm((NCH, CW, users), BF16),
        vm((NCH, 128, users), BF16), vm((NCH, 128, users), BF16), vm((NCH, 3, 32, users), BF16),
        vm((NCH, 32, users), BF16), vm((NCH, 32, users), BF16),
    ]
    for lead in ((2, 2), (2, 2), (2, 2), (2, 4), (NCH, 2), (NCH, 2), (NCH, 2), (NCH, 4)):
        scratch += [vm(lead + (CW, half), I16), vm(lead + (1, half), F32)]
    scratch += [
        vm((2, CW, half), F32),
        vm((64, 1024), F32), vm((7, 8, 1024), F32), vm((16, 64, 1024), F32),
        dma((NCH, 9)), dma((NCH, 9)), dma((NCH, 12)), dma((NCH, 12)), dma((NCH, 8)), dma((NCH, 8)),
        dma((29,)), dma((29,)), dma,
    ]
    return pl.pallas_call(
        kernel,
        out_shape=(jax.ShapeDtypeStruct((NCH, CW, half), F32), jax.ShapeDtypeStruct((16, 64, 1024), F32)),
        in_specs=[pl.BlockSpec(memory_space=pltpu.SMEM), pl.BlockSpec(memory_space=pl.ANY)],
        out_specs=(pl.BlockSpec(memory_space=pltpu.VMEM), pl.BlockSpec(memory_space=pltpu.VMEM)),
        scratch_shapes=scratch,
        compiler_params=pltpu.CompilerParams(collective_id=1, has_side_effects=True, vmem_limit_bytes=62 * 2**20),
    )(panel_ids, history)


def local(history, ridge, pivot_inverse, panel_ids):
    group_items = history.shape[1]
    block_rows = group_items // 8
    total_rows = history.shape[0] * 8
    first_row = lax.axis_index(("srow", "scol")) * group_items + lax.axis_index("users") * block_rows
    items_here = first_row + jnp.arange(block_rows, dtype=jnp.int32)
    ridge_here = lax.dynamic_slice_in_dim(ridge, first_row, block_rows)
    gram, piv = run(history, panel_ids)
    gram = gram.reshape(2, 1024, block_rows)
    piv = piv.reshape(1024, 1024) / float(total_rows)
    cols = panel_ids[:, None] * 1024 + jnp.arange(1024, dtype=jnp.int32)[None]
    on_diagonal = items_here[None, None, :] == cols[:, :, None]
    gram = gram / float(total_rows) + jnp.where(on_diagonal, ridge_here[None, None, :], 0.0)
    hi = lax.Precision.HIGHEST
    factor_a = lax.dot_general(gram[0], pivot_inverse[0], (((0,), (0,)), ((), ())), precision=hi)
    schur = gram[1] - lax.dot_general(piv, factor_a, (((1,), (1,)), ((), ())), precision=hi)
    factor_b = lax.dot_general(schur, pivot_inverse[1], (((0,), (0,)), ((), ())), precision=hi)
    return factor_a[None], factor_b[None]


def solution(mesh):
    return jax.shard_map(
        local,
        mesh=mesh,
        in_specs=(P("users", ("srow", "scol")), P(), P(), P()),
        out_specs=(P(("srow", "scol"), "users", None), P(("srow", "scol"), "users", None)),
        check_vma=False,
    )
```

```python
import functools

import jax
import jax.numpy as jnp
from jax import lax
from jax.experimental import pallas as pl
from jax.experimental.pallas import tpu as pltpu
from jax.sharding import PartitionSpec as P

MESH = pl.DeviceIdType.MESH
F32 = jnp.float32
BF16 = jnp.bfloat16
I16 = jnp.int16

CW = 256
KINDS = "ZZXZXZXZ"
NCH = len(KINDS)
HALF = NCH // 2
ORDER = {k: [c for c in range(NCH) if KINDS[c] == k] for k in "ZX"}
NTH = [ORDER[k].index(c) for c, k in enumerate(KINDS)]
TOP = 32767.0


def encode(v):
    top = jnp.maximum(jnp.max(jnp.abs(v), axis=0, keepdims=True), 1e-30)
    q = jnp.round(v * (TOP / top)).astype(jnp.int32).astype(I16)
    return q, top * (1.0 / TOP)


def decode(q, s):
    return q.astype(jnp.int32).astype(F32) * s


def split(v):
    hi = v.astype(BF16)
    return hi, (v - hi.astype(F32)).astype(BF16)


def dot3(a, b, dims=(((1,), (0,)), ((), ()))):
    (ah, al), (bh, bl) = a, b
    d = functools.partial(lax.dot_general, dimension_numbers=dims, preferred_element_type=F32)
    return d(ah, bh) + (d(ah, bl) + d(al, bh))


def kernel(pid, hist_hbm, ridge, pinv_hbm, fa_hbm, fb_hbm,
           hist, pT, msk, cor, comb, yin, mid, xin,
           q2z, s2z, qdz, sdz, qaz, saz, qxz, sxz,
           q2x, s2x, qdx, sdx, qax, sax, qxx, sxx,
           r2z, t2z, rdz, tdz, raz, taz, rxz, txz,
           r2x, t2x, rdx, tdx, rax, tax, rxx, txx,
           keep, pvp, pvr, pvs, gram, cross, fa, fb, pinv, ahi, alo,
           bs, br, zs, zr, xs, xr, ps, pr, hs, qs, os):
    u = lax.axis_index("users")
    y = lax.axis_index("srow")
    s = lax.axis_index("scol")
    z, xl = u // 2, u % 2
    xh, co = s // 2, s % 2
    g = y * 4 + s
    users, items = hist.shape
    total_rows = float(users * 8)
    zc = items // 4
    half = zc // 2
    first_item = g * items + u * half
    bufs = {"Z": dict(q2=(q2z, s2z), qd=(qdz, sdz), qa=(qaz, saz), qx=(qxz, sxz),
                      r2=(r2z, t2z), rd=(rdz, tdz), ra=(raz, taz), rx=(rxz, txz)),
            "X": dict(q2=(q2x, s2x), qd=(qdx, sdx), qa=(qax, sax), qx=(qxx, sxx),
                      r2=(r2x, t2x), rd=(rdx, tdx), ra=(rax, tax), rx=(rxx, txx))}

    def at(z_=None, xl_=None, y_=None, xh_=None, co_=None):
        zz = z if z_ is None else z_
        ll = xl if xl_ is None else xl_
        yy = y if y_ is None else y_
        hh = xh if xh_ is None else xh_
        cc = co if co_ is None else co_
        return (zz * 2 + ll, yy, hh * 2 + cc)

    up, dn, op = (z + 1) % 4, (z + 3) % 4, (z + 2) % 4
    p_up, p_dn, p_x = at(z_=up), at(z_=dn), at(xl_=1 - xl)
    p_core, p_xh = at(co_=1 - co), at(xh_=1 - xh)
    p_y = [at(y_=(y + d) % 4) for d in (1, 2, 3)]
    p_u = [((u + d) % 8, y, s) for d in range(1, 8)]
    p_ux = [((u + d) % 8, y, (xh + b) % 2 * 2 + co) for d in range(8) for b in range(2)][1:]

    load = pltpu.make_async_copy(hist_hbm, hist, hs)
    load.start()
    barrier = pltpu.get_barrier_semaphore()
    everyone = [p_core] + p_y + p_ux
    for peer in everyone:
        pl.semaphore_signal(barrier, inc=1, device_id=peer, device_id_type=MESH)
    pl.semaphore_wait(barrier, len(everyone))
    load.wait()

    live, descs, waited = {}, {}, set()

    def send(key, src, dst, ss, rs, peer):
        c = pltpu.make_async_remote_copy(src, dst, ss, rs, device_id=peer, device_id_type=MESH)
        c.start()
        live[key] = descs[key] = c

    def got(key):
        live.pop(key).wait_recv()

    def wait_sent(key):
        if key in descs and key not in waited:
            waited.add(key)
            descs[key].wait_send()

    def sendq(key, src, dst, ss, rs, i, peer):
        for n in (0, 1):
            send(key + (n,), src[n], dst[n], ss.at[i + n], rs.at[i + n], peer)

    def gotq(key):
        for n in (0, 1):
            got(key + (n,))

    def sentq(key):
        for n in (0, 1):
            wait_sent(key + (n,))

    def bc1(c):
        k, j = divmod(c, HALF)
        v = None
        for b in range(items // 1024):
            mine = (pid[k] == 4 * g + b).astype(F32).astype(BF16)
            term = hist[:, pl.ds(b * 1024 + j * CW, CW)] * mine
            v = term if v is None else v + term
        wait_sent(("b0", c - 3))
        msk[c % 3] = v.T
        send(("b0", c), msk.at[c % 3, pl.ds(pl.multiple_of((1 - co) * 128, 128), 128)], cor.at[c], bs.at[c, 0], br.at[c, 0], p_core)

    def bc2(c):
        got(("b0", c))
        for d in (1, 2, 3):
            wait_sent(("b1", c - 3, d))
        comb[c % 3] = msk[c % 3, pl.ds(pl.multiple_of(co * 128, 128), 128)] + cor[c]
        for d in (1, 2, 3):
            yy = (y + d) % 4
            send(("b1", c, d), comb.at[c % 3, pl.ds(pl.multiple_of(yy * 32, 32), 32)], yin.at[c, d - 1],
                 bs.at[c, d], br.at[c, d], p_y[d - 1])

    def bc3(c):
        for d in (1, 2, 3):
            got(("b1", c, d))
        mid[c] = comb[c % 3, pl.ds(pl.multiple_of(y * 32, 32), 32)] + yin[c, 0] + yin[c, 1] + yin[c, 2]
        send(("b2", c), mid.at[c], xin.at[c], bs.at[c, 4], br.at[c, 4], p_xh)

    def bc4(c):
        got(("b2", c))
        here = pl.ds(pl.multiple_of(co * 128 + y * 32, 32), 32)
        pT[c, here] = mid[c] + xin[c]
        for d in (1, 2, 3):
            send(("b3", c, d), pT.at[c, here], pT.at[c, here], bs.at[c, 4 + d], br.at[c, 4 + d], p_y[d - 1])

    def bc5(c):
        for d in (1, 2, 3):
            got(("b3", c, d))
        here = pl.ds(pl.multiple_of(co * 128, 128), 128)
        send(("b4", c), pT.at[c, here], pT.at[c, here], bs.at[c, 8], br.at[c, 8], p_core)

    def bc6(c):
        got(("b4", c))

    def tiles(c, lane0, width, adds, out):
        def one(t, carry):
            lane = pl.multiple_of(lane0 + t * 256, 256)
            o = pl.multiple_of(t * 256, 256)
            v = jnp.dot(pT[c], hist[:, pl.ds(lane, 256)], preferred_element_type=F32)
            for q, sc in adds:
                v = v + decode(q[:, pl.ds(o, 256)], sc[:, pl.ds(o, 256)])
            out(o, v)
            return carry
        if width == 256:
            one(0, 0)
        else:
            lax.fori_loop(0, width // 256, one, 0)

    def coded(buf):
        def out(o, v):
            q, sc = encode(v)
            buf[0][:, pl.ds(o, 256)] = q
            buf[1][:, pl.ds(o, 256)] = sc
        return out

    def final(c):
        k, j = divmod(c, HALF)

        def out(o, v):
            r = lax.broadcasted_iota(jnp.int32, v.shape, 0) + (pid[k] * 1024 + j * CW)
            i = lax.broadcasted_iota(jnp.int32, v.shape, 1) + (first_item + o)
            v = v * (1.0 / total_rows) + jnp.where(r == i, ridge[:, pl.ds(o, 256)], 0.0)
            gram[c % HALF, pl.ds(o, 256)] = v.T
        return out

    def width(c):
        return half if KINDS[c] == "Z" else half // 2

    def pick(c, name, *ix):
        lead = NTH[c] % 2 if name[0] == "q" else NTH[c]
        return tuple(b.at[(lead,) + ix] for b in bufs[KINDS[c]][name])

    def before(c):
        n = NTH[c]
        return ORDER[KINDS[c]][n - 2] if n >= 2 else -1

    def lane(c, zz, h):
        if KINDS[c] == "Z":
            return zz * zc + h * half
        return zz * zc + xl * half + h * (half // 2)

    def xadd(c, i, h):
        if KINDS[c] == "Z":
            return []
        w = half // 2
        q, sc = pick(c, "rx", i)
        return [(q.at[:, pl.ds(h * w, w)], sc.at[:, pl.ds(h * w, w)])]

    def x1(c, some=(0, 1, 2, 3)):
        for i in some:
            zz = (op, up, dn, z)[i]
            sentq(("x", before(c), i))
            tiles(c, zz * zc + (1 - xl) * half, half, [], coded(pick(c, "qx", i)))
            sendq(("x", c, i), pick(c, "qx", i), pick(c, "rx", i), xs.at[c], xr.at[c], 2 * i, p_x)

    def step(c, name, dst, h, zz, i, adds, ss, peer):
        sentq((name, before(c), h))
        tiles(c, lane(c, zz, h), width(c), xadd(c, i, h) + adds, coded(pick(c, name, h)))
        sendq((name, c, h), pick(c, name, h), pick(c, dst, h), zs.at[c], zr.at[c], ss + 2 * h, peer)

    def z_first(c):
        if KINDS[c] == "X":
            gotq(("x", c, 0))
        for h, peer in ((0, p_dn), (1, p_up)):
            step(c, "q2", "r2", h, op, 0, [], 0, peer)

    def z_direct(c):
        if KINDS[c] == "X":
            gotq(("x", c, 1))
            gotq(("x", c, 2))
        for h, zz, i, peer in ((0, up, 1, p_up), (1, dn, 2, p_dn)):
            step(c, "qd", "rd", h, zz, i, [], 4, peer)

    def z_pass(c):
        for h, zz, i, peer in ((0, dn, 2, p_dn), (1, up, 1, p_up)):
            gotq(("q2", c, h))
            step(c, "qa", "ra", h, zz, i, [pick(c, "r2", h)], 8, peer)

    def z_last(c):
        if KINDS[c] == "X":
            gotq(("x", c, 3))
        for h in (0, 1):
            gotq(("qd", c, h))
            gotq(("qa", c, h))
        if KINDS[c] == "X":
            for h in (0, 1):
                def out(o, v, h=h):
                    final(c)(h * width(c) + o, v)
                tiles(c, lane(c, z, h), width(c), xadd(c, 3, h) + [pick(c, "rd", h), pick(c, "ra", h)], out)
            return
        sentq(("x", before(c), 0))
        tiles(c, lane(c, z, 1 - xl), half, [pick(c, "rd", 1 - xl), pick(c, "ra", 1 - xl)], coded(pick(c, "qx")))
        sendq(("x", c, 0), pick(c, "qx"), pick(c, "rx"), xs.at[c], xr.at[c], 0, p_x)

        def out(o, v):
            keep[NTH[c] % 2, :, pl.ds(o, 256)] = v
        tiles(c, lane(c, z, xl), half, [pick(c, "rd", xl), pick(c, "ra", xl)], out)

    def x_last(c):
        gotq(("x", c, 0))
        q, sc = pick(c, "rx")

        def one(t, carry):
            o = pl.multiple_of(t * 256, 256)
            final(c)(o, keep[NTH[c] % 2, :, pl.ds(o, 256)] + decode(q[:, pl.ds(o, 256)], sc[:, pl.ds(o, 256)]))
            return carry
        lax.fori_loop(0, half // 256, one, 0)

    def pv1():
        rows = pT[HALF + g // 4, pl.ds(pl.multiple_of((g % 4) * 64, 64), 64)]
        for j in range(HALF):
            pvp[:, pl.ds(j * CW, CW)] = lax.dot_general(
                rows, pT[j], (((1,), (1,)), ((), ())), preferred_element_type=F32)
        for d in range(1, 8):
            uu = (u + d) % 8
            send(("p0", d), pvp.at[pl.ds(pl.multiple_of(uu * 8, 8), 8)], pvr.at[d - 1], ps.at[d - 1], pr.at[d - 1], p_u[d - 1])

    def pv2():
        v = pvp[pl.ds(pl.multiple_of(u * 8, 8), 8)]
        for d in range(1, 8):
            got(("p0", d))
            v = v + pvr[d - 1]
        here = pl.ds(pl.multiple_of(u * 8, 8), 8)
        pvs[g, here] = v * (1.0 / total_rows)
        for d, peer in enumerate(p_ux):
            send(("p1", d), pvs.at[g, here], pvs.at[g, here], ps.at[7 + d], pr.at[7 + d], peer)

    def pv3():
        for d in range(15):
            got(("p1", d))
        for d in (1, 2, 3):
            for b in (0, 1):
                gg = y * 4 + b * 2 + co
                send(("p2", d, b), pvs.at[gg], pvs.at[gg], ps.at[20 + 2 * d + b], pr.at[20 + 2 * d + b], p_y[d - 1])

    def pv4():
        for d in (1, 2, 3):
            for b in (0, 1):
                got(("p2", d, b))
        for b in range(8):
            gg = b * 2 + co
            send(("p3", b), pvs.at[gg], pvs.at[gg], ps.at[28 + b], pr.at[28 + b], p_core)

    def pv5():
        for b in range(8):
            got(("p3", b))

    def fetch(c):
        k, j = divmod(c, HALF)
        return pltpu.make_async_copy(pinv_hbm.at[k, pl.ds(j * CW, CW)], pinv.at[c % 2], qs.at[c % 2])

    def factor(c):
        k, j = divmod(c, HALF)
        acc = (fa, fb)[k]
        d = gram[j] if k == 0 else gram[j] - cross[j]
        hi, lo = split(d)
        ahi[:, pl.ds(0, CW)] = hi
        alo[:, pl.ds(0, CW)] = lo
        fetch(c).wait()

        def one(t, carry):
            here = pl.ds(pl.multiple_of(t * 256, 256), 256)
            v = dot3((ahi[:, pl.ds(0, CW)], alo[:, pl.ds(0, CW)]), split(pinv[c % 2, :, here]))
            acc[:, here] = v if j == 0 else acc[:, here] + v
            return carry
        lax.fori_loop(0, 4, one, 0)
        if c + 2 < NCH:
            fetch(c + 2).start()

    def out_copy(k):
        return pltpu.make_async_copy((fa, fb)[k], (fa_hbm, fb_hbm)[k], os.at[k])

    def crossing():
        out_copy(0).start()

        def part(t, carry):
            here = pl.ds(pl.multiple_of(t * 256, 256), 256)
            hi, lo = split(fa[:, here])
            ahi[:, here] = hi
            alo[:, here] = lo
            return carry
        lax.fori_loop(0, 4, part, 0)

        def one(t, carry):
            rows = pvs[pl.ds(t * 4, 4)].reshape(256, 1024)
            cross[t] = dot3((ahi[...], alo[...]), split(rows), (((1,), (1,)), ((), ())))
            return carry
        lax.fori_loop(0, 4, one, 0)

    fetch(0).start()
    fetch(1).start()

    bc = (bc1, bc2, bc3, bc4, bc5, bc6)

    def slot(t):
        for n in reversed(range(6)):
            if 0 <= t - n < NCH:
                bc[n](t - n)

    for t in range(6):
        slot(t)
    slots = list(range(6, NCH + 5))
    pvq = [pv1, pv2, pv3, pv4, pv5]
    stages = {"Z": ((z_first, z_direct), (z_pass,), (z_last,), (x_last,)),
              "X": ((x1,), (z_first, z_direct), (z_pass,), (z_last,))}
    done = 0
    for i in range(NCH + 3):
        for lag in range(4):
            c = i - lag
            if not 0 <= c < NCH:
                continue
            for f in stages[KINDS[c]][lag]:
                f(c)
                if slots:
                    slot(slots.pop(0))
            if lag == 3 and c < HALF:
                factor(c)
        if not slots and pvq:
            pvq.pop(0)()
        if i == NCH:
            while pvq:
                pvq.pop(0)()
            crossing()
        if i >= NCH:
            while done < HALF and HALF + done + 3 <= i:
                factor(HALF + done)
                done += 1
    out_copy(1).start()
    for key in descs:
        wait_sent(key)
    out_copy(0).wait()
    out_copy(1).wait()


def run(history, ridge, pivot_inverse, panel_ids):
    users, items = history.shape
    half = items // 8
    vm = pltpu.VMEM
    dma = pltpu.SemaphoreType.DMA
    nz, nx = len(ORDER["Z"]), len(ORDER["X"])
    scratch = [
        vm((users, items), BF16), vm((NCH, CW, users), BF16), vm((3, CW, users), BF16),
        vm((NCH, 128, users), BF16), vm((3, 128, users), BF16), vm((NCH, 3, 32, users), BF16),
        vm((NCH, 32, users), BF16), vm((NCH, 32, users), BF16),
    ]
    for lead, w in (((2, 2), half), ((2, 2), half), ((2, 2), half), ((2,), half),
                    ((2, 2), half // 2), ((2, 2), half // 2), ((2, 2), half // 2), ((2, 4), half),
                    ((nz, 2), half), ((nz, 2), half), ((nz, 2), half), ((nz,), half),
                    ((nx, 2), half // 2), ((nx, 2), half // 2), ((nx, 2), half // 2), ((nx, 4), half)):
        scratch += [vm(lead + (CW, w), I16), vm(lead + (1, w), F32)]
    scratch += [
        vm((2, CW, half), F32),
        vm((64, 1024), F32), vm((7, 8, 1024), F32), vm((16, 64, 1024), F32),
        vm((HALF, half, CW), F32), vm((HALF, half, CW), F32),
        vm((half, 1024), F32), vm((half, 1024), F32), vm((2, CW, 1024), F32),
        vm((half, 1024), BF16), vm((half, 1024), BF16),
        dma((NCH, 9)), dma((NCH, 9)), dma((NCH, 12)), dma((NCH, 12)), dma((NCH, 8)), dma((NCH, 8)),
        dma((36,)), dma((36,)), dma, dma((2,)), dma((2,)),
    ]
    hbm = pl.BlockSpec(memory_space=pl.ANY)
    return pl.pallas_call(
        kernel,
        out_shape=(jax.ShapeDtypeStruct((half, 1024), F32),) * 2,
        in_specs=[pl.BlockSpec(memory_space=pltpu.SMEM), hbm, pl.BlockSpec(memory_space=pltpu.VMEM), hbm],
        out_specs=(hbm, hbm),
        scratch_shapes=scratch,
        compiler_params=pltpu.CompilerParams(collective_id=1, has_side_effects=True, vmem_limit_bytes=62 * 2**20),
    )(panel_ids, history, ridge, pivot_inverse)


def local(history, ridge, pivot_inverse, panel_ids):
    group_items = history.shape[1]
    block_rows = group_items // 8
    first_row = lax.axis_index(("srow", "scol")) * group_items + lax.axis_index("users") * block_rows
    ridge_here = lax.dynamic_slice_in_dim(ridge, first_row, block_rows)
    factor_a, factor_b = run(history, ridge_here[None], pivot_inverse, panel_ids)
    return factor_a[None], factor_b[None]


def solution(mesh):
    return jax.shard_map(
        local,
        mesh=mesh,
        in_specs=(P("users", ("srow", "scol")), P(), P(), P()),
        out_specs=(P(("srow", "scol"), "users", None), P(("srow", "scol"), "users", None)),
        check_vma=False,
    )
```

```python
import functools

import jax
import jax.numpy as jnp
from jax import lax
from jax.experimental import pallas as pl
from jax.experimental.pallas import tpu as pltpu
from jax.sharding import PartitionSpec as P

MESH = pl.DeviceIdType.MESH
F32 = jnp.float32
BF16 = jnp.bfloat16
I16 = jnp.int16

CW = 256
KINDS = "ZZXZXZXZ"
NCH = len(KINDS)
HALF = NCH // 2
ORDER = {k: [c for c in range(NCH) if KINDS[c] == k] for k in "ZX"}
NTH = [ORDER[k].index(c) for c, k in enumerate(KINDS)]
TOP = 32767.0


def encode(v):
    top = jnp.maximum(jnp.max(jnp.abs(v), axis=0, keepdims=True), 1e-30)
    q = jnp.round(v * (TOP / top)).astype(jnp.int32).astype(I16)
    return q, top * (1.0 / TOP)


def decode(q, s):
    return q.astype(jnp.int32).astype(F32) * s


def split(v):
    hi = v.astype(BF16)
    return hi, (v - hi.astype(F32)).astype(BF16)


def dot3(a, b, dims=(((1,), (0,)), ((), ()))):
    (ah, al), (bh, bl) = a, b
    d = functools.partial(lax.dot_general, dimension_numbers=dims, preferred_element_type=F32)
    return d(ah, bh) + (d(ah, bl) + d(al, bh))


def kernel(pid, hist_hbm, ridge, pinv_hbm, fa_hbm, fb_hbm,
           hist, pT, msk, cor, comb, yin, mid, xin,
           q2z, s2z, qdz, sdz, qaz, saz, qxz, sxz,
           q2x, s2x, qdx, sdx, qax, sax, qxx, sxx,
           r2z, t2z, rdz, tdz, raz, taz, rxz, txz,
           r2x, t2x, rdx, tdx, rax, tax, rxx, txx,
           keep, pvp, pvr, pvs, gram, cross, fa, fb, pinv, ahi, alo,
           bs, br, zs, zr, xs, xr, ps, pr, hs, qs, os):
    u = lax.axis_index("users")
    y = lax.axis_index("srow")
    s = lax.axis_index("scol")
    z, xl = u // 2, u % 2
    xh, co = s // 2, s % 2
    g = y * 4 + s
    users, items = hist.shape
    total_rows = float(users * 8)
    zc = items // 4
    half = zc // 2
    first_item = g * items + u * half
    bufs = {"Z": dict(q2=(q2z, s2z), qd=(qdz, sdz), qa=(qaz, saz), qx=(qxz, sxz),
                      r2=(r2z, t2z), rd=(rdz, tdz), ra=(raz, taz), rx=(rxz, txz)),
            "X": dict(q2=(q2x, s2x), qd=(qdx, sdx), qa=(qax, sax), qx=(qxx, sxx),
                      r2=(r2x, t2x), rd=(rdx, tdx), ra=(rax, tax), rx=(rxx, txx))}

    def at(z_=None, xl_=None, y_=None, xh_=None, co_=None):
        zz = z if z_ is None else z_
        ll = xl if xl_ is None else xl_
        yy = y if y_ is None else y_
        hh = xh if xh_ is None else xh_
        cc = co if co_ is None else co_
        return (zz * 2 + ll, yy, hh * 2 + cc)

    up, dn, op = (z + 1) % 4, (z + 3) % 4, (z + 2) % 4
    p_up, p_dn, p_x = at(z_=up), at(z_=dn), at(xl_=1 - xl)
    p_core, p_xh = at(co_=1 - co), at(xh_=1 - xh)
    p_y = [at(y_=(y + d) % 4) for d in (1, 2, 3)]
    p_u = [((u + d) % 8, y, s) for d in range(1, 8)]
    p_ux = [((u + d) % 8, y, (xh + b) % 2 * 2 + co) for d in range(8) for b in range(2)][1:]

    load = pltpu.make_async_copy(hist_hbm, hist, hs)
    load.start()
    barrier = pltpu.get_barrier_semaphore()
    everyone = [p_core] + p_y + p_ux
    for peer in everyone:
        pl.semaphore_signal(barrier, inc=1, device_id=peer, device_id_type=MESH)
    pl.semaphore_wait(barrier, len(everyone))
    load.wait()

    live, descs, waited = {}, {}, set()

    def send(key, src, dst, ss, rs, peer):
        c = pltpu.make_async_remote_copy(src, dst, ss, rs, device_id=peer, device_id_type=MESH)
        c.start()
        live[key] = descs[key] = c

    def got(key):
        live.pop(key).wait_recv()

    def wait_sent(key):
        if key in descs and key not in waited:
            waited.add(key)
            descs[key].wait_send()

    def sendq(key, src, dst, ss, rs, i, peer):
        for n in (0, 1):
            send(key + (n,), src[n], dst[n], ss.at[i + n], rs.at[i + n], peer)

    def gotq(key):
        for n in (0, 1):
            got(key + (n,))

    def sentq(key):
        for n in (0, 1):
            wait_sent(key + (n,))

    def bc1(c):
        k, j = divmod(c, HALF)
        v = None
        for b in range(items // 1024):
            mine = (pid[k] == 4 * g + b).astype(F32).astype(BF16)
            term = hist[:, pl.ds(b * 1024 + j * CW, CW)] * mine
            v = term if v is None else v + term
        wait_sent(("b0", c - 3))
        msk[c % 3] = v.T
        send(("b0", c), msk.at[c % 3, pl.ds(pl.multiple_of((1 - co) * 128, 128), 128)], cor.at[c], bs.at[c, 0], br.at[c, 0], p_core)

    def bc2(c):
        got(("b0", c))
        for d in (1, 2, 3):
            wait_sent(("b1", c - NCH, d))
        comb[c] = msk[c % 3, pl.ds(pl.multiple_of(co * 128, 128), 128)] + cor[c]
        for d in (1, 2, 3):
            yy = (y + d) % 4
            send(("b1", c, d), comb.at[c, pl.ds(pl.multiple_of(yy * 32, 32), 32)], yin.at[c, d - 1],
                 bs.at[c, d], br.at[c, d], p_y[d - 1])

    def bc3(c):
        for d in (1, 2, 3):
            got(("b1", c, d))
        mid[c] = comb[c, pl.ds(pl.multiple_of(y * 32, 32), 32)] + yin[c, 0] + yin[c, 1] + yin[c, 2]
        send(("b2", c), mid.at[c], xin.at[c], bs.at[c, 4], br.at[c, 4], p_xh)

    def bc4(c):
        got(("b2", c))
        here = pl.ds(pl.multiple_of(co * 128 + y * 32, 32), 32)
        pT[c, here] = mid[c] + xin[c]
        for d in (1, 2, 3):
            send(("b3", c, d), pT.at[c, here], pT.at[c, here], bs.at[c, 4 + d], br.at[c, 4 + d], p_y[d - 1])

    def bc5(c):
        for d in (1, 2, 3):
            got(("b3", c, d))
        here = pl.ds(pl.multiple_of(co * 128, 128), 128)
        send(("b4", c), pT.at[c, here], pT.at[c, here], bs.at[c, 8], br.at[c, 8], p_core)

    def bc6(c):
        got(("b4", c))

    def tiles(c, lane0, width, adds, out):
        def one(t, carry):
            lane = pl.multiple_of(lane0 + t * 256, 256)
            o = pl.multiple_of(t * 256, 256)
            v = jnp.dot(pT[c], hist[:, pl.ds(lane, 256)], preferred_element_type=F32)
            for q, sc in adds:
                v = v + decode(q[:, pl.ds(o, 256)], sc[:, pl.ds(o, 256)])
            out(o, v)
            return carry
        if width == 256:
            one(0, 0)
        else:
            lax.fori_loop(0, width // 256, one, 0)

    def coded(buf):
        def out(o, v):
            q, sc = encode(v)
            buf[0][:, pl.ds(o, 256)] = q
            buf[1][:, pl.ds(o, 256)] = sc
        return out

    def final(c):
        k, j = divmod(c, HALF)

        def out(o, v):
            r = lax.broadcasted_iota(jnp.int32, v.shape, 0) + (pid[k] * 1024 + j * CW)
            i = lax.broadcasted_iota(jnp.int32, v.shape, 1) + (first_item + o)
            v = v * (1.0 / total_rows) + jnp.where(r == i, ridge[:, pl.ds(o, 256)], 0.0)
            gram[c % HALF, pl.ds(o, 256)] = v.T
        return out

    def width(c):
        return half if KINDS[c] == "Z" else half // 2

    def pick(c, name, *ix):
        lead = NTH[c] % 2 if name[0] == "q" else NTH[c]
        return tuple(b.at[(lead,) + ix] for b in bufs[KINDS[c]][name])

    def before(c):
        n = NTH[c]
        return ORDER[KINDS[c]][n - 2] if n >= 2 else -1

    def lane(c, zz, h):
        if KINDS[c] == "Z":
            return zz * zc + h * half
        return zz * zc + xl * half + h * (half // 2)

    def xadd(c, i, h):
        if KINDS[c] == "Z":
            return []
        w = half // 2
        q, sc = pick(c, "rx", i)
        return [(q.at[:, pl.ds(h * w, w)], sc.at[:, pl.ds(h * w, w)])]

    def x1(c, some=(0, 1, 2, 3)):
        for i in some:
            zz = (op, up, dn, z)[i]
            sentq(("x", before(c), i))
            tiles(c, zz * zc + (1 - xl) * half, half, [], coded(pick(c, "qx", i)))
            sendq(("x", c, i), pick(c, "qx", i), pick(c, "rx", i), xs.at[c], xr.at[c], 2 * i, p_x)

    def step(c, name, dst, h, zz, i, adds, ss, peer):
        sentq((name, before(c), h))
        tiles(c, lane(c, zz, h), width(c), xadd(c, i, h) + adds, coded(pick(c, name, h)))
        sendq((name, c, h), pick(c, name, h), pick(c, dst, h), zs.at[c], zr.at[c], ss + 2 * h, peer)

    def z_first(c):
        if KINDS[c] == "X":
            gotq(("x", c, 0))
        for h, peer in ((0, p_dn), (1, p_up)):
            step(c, "q2", "r2", h, op, 0, [], 0, peer)

    def z_direct(c):
        if KINDS[c] == "X":
            gotq(("x", c, 1))
            gotq(("x", c, 2))
        for h, zz, i, peer in ((0, up, 1, p_up), (1, dn, 2, p_dn)):
            step(c, "qd", "rd", h, zz, i, [], 4, peer)

    def z_pass(c):
        for h, zz, i, peer in ((0, dn, 2, p_dn), (1, up, 1, p_up)):
            gotq(("q2", c, h))
            step(c, "qa", "ra", h, zz, i, [pick(c, "r2", h)], 8, peer)

    def z_last(c):
        if KINDS[c] == "X":
            gotq(("x", c, 3))
        for h in (0, 1):
            gotq(("qd", c, h))
            gotq(("qa", c, h))
        if KINDS[c] == "X":
            for h in (0, 1):
                def out(o, v, h=h):
                    final(c)(h * width(c) + o, v)
                tiles(c, lane(c, z, h), width(c), xadd(c, 3, h) + [pick(c, "rd", h), pick(c, "ra", h)], out)
            return
        sentq(("x", before(c), 0))
        tiles(c, lane(c, z, 1 - xl), half, [pick(c, "rd", 1 - xl), pick(c, "ra", 1 - xl)], coded(pick(c, "qx")))
        sendq(("x", c, 0), pick(c, "qx"), pick(c, "rx"), xs.at[c], xr.at[c], 0, p_x)

        def out(o, v):
            keep[NTH[c] % 2, :, pl.ds(o, 256)] = v
        tiles(c, lane(c, z, xl), half, [pick(c, "rd", xl), pick(c, "ra", xl)], out)

    def x_last(c):
        gotq(("x", c, 0))
        q, sc = pick(c, "rx")

        def one(t, carry):
            o = pl.multiple_of(t * 256, 256)
            final(c)(o, keep[NTH[c] % 2, :, pl.ds(o, 256)] + decode(q[:, pl.ds(o, 256)], sc[:, pl.ds(o, 256)]))
            return carry
        lax.fori_loop(0, half // 256, one, 0)

    def pv1():
        rows = pT[HALF + g // 4, pl.ds(pl.multiple_of((g % 4) * 64, 64), 64)]
        for j in range(HALF):
            pvp[:, pl.ds(j * CW, CW)] = lax.dot_general(
                rows, pT[j], (((1,), (1,)), ((), ())), preferred_element_type=F32)
        for d in range(1, 8):
            uu = (u + d) % 8
            send(("p0", d), pvp.at[pl.ds(pl.multiple_of(uu * 8, 8), 8)], pvr.at[d - 1], ps.at[d - 1], pr.at[d - 1], p_u[d - 1])

    def pv2():
        v = pvp[pl.ds(pl.multiple_of(u * 8, 8), 8)]
        for d in range(1, 8):
            got(("p0", d))
            v = v + pvr[d - 1]
        here = pl.ds(pl.multiple_of(u * 8, 8), 8)
        pvs[g, here] = v * (1.0 / total_rows)
        for d, peer in enumerate(p_ux):
            send(("p1", d), pvs.at[g, here], pvs.at[g, here], ps.at[7 + d], pr.at[7 + d], peer)

    def pv3():
        for d in range(15):
            got(("p1", d))
        for d in (1, 2, 3):
            for b in (0, 1):
                gg = y * 4 + b * 2 + co
                send(("p2", d, b), pvs.at[gg], pvs.at[gg], ps.at[20 + 2 * d + b], pr.at[20 + 2 * d + b], p_y[d - 1])

    def pv4():
        for d in (1, 2, 3):
            for b in (0, 1):
                got(("p2", d, b))
        for b in range(8):
            gg = b * 2 + co
            send(("p3", b), pvs.at[gg], pvs.at[gg], ps.at[28 + b], pr.at[28 + b], p_core)

    def pv5():
        for b in range(8):
            got(("p3", b))

    def fetch(c):
        k, j = divmod(c, HALF)
        return pltpu.make_async_copy(pinv_hbm.at[k, pl.ds(j * CW, CW)], pinv.at[c % 2], qs.at[c % 2])

    def factor(c):
        k, j = divmod(c, HALF)
        acc = (fa, fb)[k]
        d = gram[j] if k == 0 else gram[j] - cross[j]
        hi, lo = split(d)
        ahi[:, pl.ds(0, CW)] = hi
        alo[:, pl.ds(0, CW)] = lo
        fetch(c).wait()

        def one(t, carry):
            here = pl.ds(pl.multiple_of(t * 256, 256), 256)
            v = dot3((ahi[:, pl.ds(0, CW)], alo[:, pl.ds(0, CW)]), split(pinv[c % 2, :, here]))
            acc[:, here] = v if j == 0 else acc[:, here] + v
            return carry
        lax.fori_loop(0, 4, one, 0)
        if c + 2 < NCH:
            fetch(c + 2).start()

    def out_copy(k):
        return pltpu.make_async_copy((fa, fb)[k], (fa_hbm, fb_hbm)[k], os.at[k])

    def crossing():
        out_copy(0).start()

        def part(t, carry):
            here = pl.ds(pl.multiple_of(t * 256, 256), 256)
            hi, lo = split(fa[:, here])
            ahi[:, here] = hi
            alo[:, here] = lo
            return carry
        lax.fori_loop(0, 4, part, 0)

        def one(t, carry):
            rows = pvs[pl.ds(t * 4, 4)].reshape(256, 1024)
            cross[t] = dot3((ahi[...], alo[...]), split(rows), (((1,), (1,)), ((), ())))
            return carry
        lax.fori_loop(0, 4, one, 0)

    fetch(0).start()
    fetch(1).start()

    bc1(0)
    for c in range(1, NCH):
        bc1(c)
        bc2(c - 1)
    bc2(NCH - 1)
    bc3(0)
    for c in range(1, NCH):
        bc3(c)
        bc4(c - 1)
    bc4(NCH - 1)
    arrive = [functools.partial(bc5, c) for c in range(2)]
    for c in range(NCH):
        arrive.append(functools.partial(bc6, c))
        if c + 2 < NCH:
            arrive.append(functools.partial(bc5, c + 2))

    def until(c):
        while arrive and arrive[0].args[0] <= c + 2:
            f = arrive.pop(0)
            f()
            if f.func is bc6 and f.args[0] == c:
                break

    pvq = [pv1, pv2, pv3, pv4, pv5]
    stages = {"Z": ((z_first, z_direct), (z_pass,), (z_last,), (x_last,)),
              "X": ((x1,), (z_first, z_direct), (z_pass,), (z_last,))}
    done = 0
    for i in range(NCH + 3):
        if any(f.func is bc6 and f.args[0] == i for f in arrive):
            until(i)
        for lag in range(4):
            c = i - lag
            if not 0 <= c < NCH:
                continue
            for f in stages[KINDS[c]][lag]:
                f(c)
                if arrive:
                    arrive.pop(0)()
                if arrive:
                    arrive.pop(0)()
            if lag == 3 and c < HALF:
                factor(c)
        if i in (2, 4, 5, 7):
            while arrive:
                arrive.pop(0)()
            pvq.pop(0)()
        if i == NCH:
            while pvq:
                pvq.pop(0)()
            crossing()
        if i >= NCH:
            while done < HALF and HALF + done + 3 <= i:
                factor(HALF + done)
                done += 1
    out_copy(1).start()
    for key in descs:
        wait_sent(key)
    out_copy(0).wait()
    out_copy(1).wait()


def run(history, ridge, pivot_inverse, panel_ids):
    users, items = history.shape
    half = items // 8
    vm = pltpu.VMEM
    dma = pltpu.SemaphoreType.DMA
    nz, nx = len(ORDER["Z"]), len(ORDER["X"])
    scratch = [
        vm((users, items), BF16), vm((NCH, CW, users), BF16), vm((3, CW, users), BF16),
        vm((NCH, 128, users), BF16), vm((NCH, 128, users), BF16), vm((NCH, 3, 32, users), BF16),
        vm((NCH, 32, users), BF16), vm((NCH, 32, users), BF16),
    ]
    for lead, w in (((2, 2), half), ((2, 2), half), ((2, 2), half), ((2,), half),
                    ((2, 2), half // 2), ((2, 2), half // 2), ((2, 2), half // 2), ((2, 4), half),
                    ((nz, 2), half), ((nz, 2), half), ((nz, 2), half), ((nz,), half),
                    ((nx, 2), half // 2), ((nx, 2), half // 2), ((nx, 2), half // 2), ((nx, 4), half)):
        scratch += [vm(lead + (CW, w), I16), vm(lead + (1, w), F32)]
    scratch += [
        vm((2, CW, half), F32),
        vm((64, 1024), F32), vm((7, 8, 1024), F32), vm((16, 64, 1024), F32),
        vm((HALF, half, CW), F32), vm((HALF, half, CW), F32),
        vm((half, 1024), F32), vm((half, 1024), F32), vm((2, CW, 1024), F32),
        vm((half, 1024), BF16), vm((half, 1024), BF16),
        dma((NCH, 9)), dma((NCH, 9)), dma((NCH, 12)), dma((NCH, 12)), dma((NCH, 8)), dma((NCH, 8)),
        dma((36,)), dma((36,)), dma, dma((2,)), dma((2,)),
    ]
    hbm = pl.BlockSpec(memory_space=pl.ANY)
    return pl.pallas_call(
        kernel,
        out_shape=(jax.ShapeDtypeStruct((half, 1024), F32),) * 2,
        in_specs=[pl.BlockSpec(memory_space=pltpu.SMEM), hbm, pl.BlockSpec(memory_space=pltpu.VMEM), hbm],
        out_specs=(hbm, hbm),
        scratch_shapes=scratch,
        compiler_params=pltpu.CompilerParams(collective_id=1, has_side_effects=True, vmem_limit_bytes=62 * 2**20),
    )(panel_ids, history, ridge, pivot_inverse)


def local(history, ridge, pivot_inverse, panel_ids):
    group_items = history.shape[1]
    block_rows = group_items // 8
    first_row = lax.axis_index(("srow", "scol")) * group_items + lax.axis_index("users") * block_rows
    ridge_here = lax.dynamic_slice_in_dim(ridge, first_row, block_rows)
    factor_a, factor_b = run(history, ridge_here[None], pivot_inverse, panel_ids)
    return factor_a[None], factor_b[None]


def solution(mesh):
    return jax.shard_map(
        local,
        mesh=mesh,
        in_specs=(P("users", ("srow", "scol")), P(), P(), P()),
        out_specs=(P(("srow", "scol"), "users", None), P(("srow", "scol"), "users", None)),
        check_vma=False,
    )
```
